32 devices in a mesh: group: 2 (over x), term: 16 (over z, y, core).
Axes of the slice: x: 2, y: 2, z: 4, core: 2. Of those that a mesh axis runs over, the one named last changes fastest.
Arguments:
- vectors: bfloat16 [6, 2048, 256], P('group', 'term'), parts along dimension 0, may hold values from -6 to 6
- left_ops: bfloat16 [1024, 256, 256], P(('group', 'term')), parts along dimension 0, may hold values from -8 to 8
- right_ops: bfloat16 [1024, 256, 256], P(('group', 'term')), parts along dimension 0, may hold values from -8 to 8
- coefficient: float32 [1024], P(('group', 'term')), parts along dimension 0, may hold values from 0.5 to 2
- source: int32 [1024], P(('group', 'term')), parts along dimension 0, may hold values from 0 to 7
- target: int32 [1024], P(('group', 'term')), parts along dimension 0, may hold values from 0 to 7
Outputs:
- sigma: float32 [6, 2048, 256], P('group', 'term'), parts along dimension 0
- residual: float32 [6, 2048, 256], P('group', 'term'), parts along dimension 0
- subspace: float32 [6, 3], P('group'), parts along dimension 0
The draws below stay inside these ranges and needn't reach their ends.
There are 2 independent parts, one for each index of `group`. The reference program is written for one: setup_inputs(seed, part) draws one part's arguments, and reference() takes and returns one part's arrays. A program takes and returns all parts, laid end to end along the dimension named above; each array names one. Nothing has to cross between parts.
All inputs are finite; a program needn't handle non-finite values.
Results may differ from the reference program's by a relative error of at most 0.0015.
Values may be sent and summed in bfloat16 or wider, within the bound.
A program may use at most 128 MiB of HBM per device.

```python
import math
import jax
import jax.numpy as jnp
import numpy as np
from jax import lax

B = 256
NSEC = 8
VECS = 3
TERM_DEV = 32
TERMS = 512
ROWS = 2048
N_TERM = 16


def dominant_matrix(key, spread):
    diag_key, off_key = jax.random.split(key, 2)
    diag = jax.random.uniform(diag_key, (TERMS, B), jnp.float32, 0.5, 2.0)
    off = jnp.clip(jax.random.normal(off_key, (TERMS, B, B), jnp.float32), -4.0, 4.0)
    eye = jnp.eye(B, dtype=jnp.float32)
    return (off * (spread / B ** 0.5) * (1.0 - eye) + diag[:, :, None] * eye).astype(jnp.bfloat16)


def draw_left_ops(key, part):
    key = jax.random.fold_in(key, 11)
    return dominant_matrix(key, 0.5)


def draw_right_ops(key, part):
    key = jax.random.fold_in(key, 23)
    return dominant_matrix(key, 0.5)


def with_ends(result, key, low, largest):
    place = [jax.random.randint(jax.random.fold_in(key, axis), (), 0, length) for axis, length in enumerate(result.shape)]
    widest = result.shape.index(max(result.shape))
    next_to = place[:widest] + [(place[widest] + 1) % result.shape[widest]] + place[widest + 1:]
    return result.at[tuple(place)].set(low).at[tuple(next_to)].set(largest)


def shard_levels(stream_key, dims, cuts, smallest, top_value):
    def one(position, parts):
        heights = jax.random.uniform(jax.random.fold_in(jax.random.fold_in(stream_key, 6), position), (parts,), jnp.float32, smallest / len(cuts), top_value / len(cuts))
        return jnp.repeat(jnp.exp(heights), dims[position] // parts).reshape((-1,) + (1,) * (len(dims) - position - 1))

    gain = one(*cuts[0])
    for cut in cuts[1:]:
        gain = gain * one(*cut)
    return gain


def rank_bounds(count, slope):
    weights = [(1 << 20) // math.isqrt(rank ** slope) + 1 for rank in range(1, count + 1)]
    scale = 1 + sum(weights) // (1 << 30)
    return np.cumsum(np.array([max(1, weight // scale) for weight in weights]))


def ranked(key, extent, number_of, skew):
    listing = rank_bounds(number_of, skew)
    ticket = jax.random.randint(jax.random.fold_in(key, 1), extent, 0, int(listing[number_of - 1]))
    rank = jnp.searchsorted(jnp.asarray(listing, jnp.int32), ticket, side="right")
    return jax.random.permutation(jax.random.fold_in(key, 2), number_of)[rank].astype(jnp.int32)


def noise(key, shape, width, reach, cuts=(), kind=jnp.bfloat16):
    factor_of = shard_levels(key, shape, cuts, -0.22, 0.18) if cuts else 1.0
    result = jax.random.normal(key, shape, jnp.float32) * width * factor_of
    return jnp.minimum(jnp.maximum(result, -reach), reach).astype(kind)


def setup_inputs(seed: int = 0, part: int = 0) -> dict:
    keys = jax.random.split(jax.random.key(seed), 7)
    part_keys = jax.random.split(jax.random.fold_in(keys[6], part), 7)
    vectors = noise(part_keys[0], (VECS, ROWS, B), 1.0, 6.0, ((1, 16),))
    left_ops = draw_left_ops(jax.random.fold_in(jax.random.fold_in(keys[6], part), 71), part)
    right_ops = draw_right_ops(jax.random.fold_in(jax.random.fold_in(keys[6], part), 71), part)
    coefficient = jnp.clip(jnp.exp(math.log(2.0) - 1.3862944 * jax.random.uniform(part_keys[3], (TERMS,), jnp.float32) ** shard_levels(part_keys[3], (TERMS,), ((0, 16),), -0.2, 0.2)), 0.5, 2.0)
    source = with_ends(ranked(part_keys[4], (TERMS,), NSEC, 2), jax.random.fold_in(part_keys[4], 3), 0, NSEC - 1).astype(jnp.int32)
    target = with_ends(jax.random.randint(part_keys[5], (TERMS,), 0, NSEC), jax.random.fold_in(part_keys[5], 1), 0, NSEC - 1).astype(jnp.int32)
    return dict(vectors=vectors, left_ops=left_ops, right_ops=right_ops, coefficient=coefficient, source=source, target=target)


def reference(vectors, left_ops, right_ops, coefficient, source, target):
    factor = NSEC / (TERM_DEV * N_TERM)
    blocks = vectors.reshape(VECS, NSEC, B, B)
    sector_ids = jnp.arange(NSEC, dtype=jnp.int32)

    def step(total, items):
        left, right, coef, src, tgt = items
        picked = jnp.take(blocks, src, axis=1)
        inner = jnp.einsum('tab,vtbc->vtac', left.astype(jnp.float32), picked.astype(jnp.float32)).astype(jnp.bfloat16)
        outer = jnp.einsum('vtac,tdc->vtad', inner.astype(jnp.float32), right.astype(jnp.float32))
        outer = outer * (coef * factor)[None, :, None, None]
        onehot = (tgt[:, None] == sector_ids[None, :]).astype(jnp.float32)
        total = total + jnp.einsum('vtad,ts->vsad', outer, onehot, precision=lax.Precision.HIGHEST)
        return (total, None)
    items = (left_ops.reshape(N_TERM, TERM_DEV, B, B), right_ops.reshape(N_TERM, TERM_DEV, B, B), coefficient.reshape(N_TERM, TERM_DEV), source.reshape(N_TERM, TERM_DEV), target.reshape(N_TERM, TERM_DEV))
    start = jnp.zeros((VECS, NSEC, B, B), jnp.float32)
    total, unused = lax.scan(step, start, items)
    sigma = total.reshape(VECS, NSEC * B, B)
    wide = vectors.astype(jnp.float32)
    proj = jnp.einsum('vrb,wrb->vw', wide, sigma, precision=lax.Precision.HIGHEST)
    norm2 = lax.optimization_barrier(jnp.sum(wide * wide, axis=(1, 2)))
    theta = jnp.diagonal(proj) / norm2
    residual = sigma - theta[:, None, None] * wide
    subspace = proj / jnp.sqrt(norm2[:, None] * norm2[None, :])
    return (sigma, residual, subspace)
```

```python
import functools

import jax
import jax.numpy as jnp
from jax import lax
from jax.experimental import pallas as pl
from jax.experimental.pallas import tpu as pltpu
from jax.sharding import PartitionSpec as P

CHAIN = 4


def axis_sizes(n):
    chips = n // 2
    inner = 1
    while (inner * 2) ** 2 <= chips:
        inner *= 2
    return chips // inner, inner


def kernel(n, na, nb, nvec, rows, width, sectors, terms,
           coef, src, tgt, vec_in, left_in, right_in,
           sigma, residual, subspace,
           x, left, right, sums, acc, cbuf, crecv, ysend, yrecv, zsend, zrecv, pbuf, precv,
           prev, last,
           load_sem, gz_s, gz_r, gy_s, gy_r, gc_s, gc_r,
           rc_s, rc_r, ry_s, ry_r, rz_s, rz_r, p_s, p_r):
    me = lax.axis_index("term")
    core = lax.rem(me, 2)
    chip = lax.div(me, 2)
    py = lax.rem(chip, nb)
    pz = lax.div(chip, nb)
    half = n // sectors // 2
    factor = sectors / (terms * n)

    def at(z, y, c):
        return (z * nb + y) * 2 + c

    def up(value, step, size):
        return lax.rem(value + step, size)

    def send(source, target, send_sem, recv_sem, device):
        copy = pltpu.make_async_remote_copy(
            src_ref=source, dst_ref=target, send_sem=send_sem, recv_sem=recv_sem,
            device_id={"term": device}, device_id_type=pl.DeviceIdType.MESH)
        return copy

    own = pltpu.make_async_copy(vec_in, x.at[chip // half, lax.rem(chip, half), core], load_sem.at[0])
    own.start()
    loads = [pltpu.make_async_copy(left_in, left, load_sem.at[1]),
             pltpu.make_async_copy(right_in, right, load_sem.at[2])]
    for copy in loads:
        copy.start()

    barrier = pltpu.get_barrier_semaphore()

    def greet(step, carry):
        pl.semaphore_signal(barrier, inc=1, device_id={"term": up(me, step, n)},
                            device_id_type=pl.DeviceIdType.MESH)
        return carry

    lax.fori_loop(1, n, greet, 0)

    ends = tuple(jnp.int32(terms) for _ in range(sectors))

    def link(t, ends):
        target = tgt[t]
        before = jnp.int32(terms)
        for s in range(sectors):
            before = jnp.where(target == s, ends[s], before)
        prev[t] = before
        return tuple(jnp.where(target == s, t, ends[s]) for s in range(sectors))

    ends = lax.fori_loop(0, terms, link, ends)
    for s in range(sectors):
        last[s] = ends[s]
    sums[terms] = jnp.zeros(sums.shape[1:], jnp.float32)

    own.wait()
    pl.semaphore_wait(barrier, n - 1)

    def block(z, y, c):
        k = z * nb + y
        return x.at[lax.div(k, half), lax.rem(k, half), c]

    sent = []

    def start(copy):
        copy.start()
        sent.append(copy)
        return copy

    def to_y_and_core(z, i):
        for o in range(1, nb):
            part = block(z, py, core)
            start(send(part, part, gy_s.at[i, o], gy_r.at[i, o], at(pz, up(py, o, nb), core)))
        part = block(z, py, core)
        start(send(part, part, gc_s.at[i, 0], gc_r.at[i, 0], at(pz, py, 1 - core)))

    def y_arrival(i):
        z = up(pz, na - i, na)
        for o in range(1, nb):
            part = block(z, up(py, nb - o, nb), core)
            send(part, part, gy_s.at[i, o], gy_r.at[i, o], me).wait_recv()
            start(send(part, part, gc_s.at[i, o], gc_r.at[i, o], at(pz, py, 1 - core)))

    for o in range(1, na):
        part = block(pz, py, core)
        start(send(part, part, gz_s.at[o], gz_r.at[o], at(up(pz, o, na), py, core)))
    to_y_and_core(pz, 0)
    for i in range(1, na):
        z = up(pz, na - i, na)
        part = block(z, py, core)
        send(part, part, gz_s.at[i], gz_r.at[i], me).wait_recv()
        to_y_and_core(z, i)
    for i in range(na):
        y_arrival(i)
    for copy in loads:
        copy.wait()
    for i in range(na):
        for o in range(nb):
            part = block(up(pz, na - i, na), up(py, nb - o, nb), 1 - core)
            send(part, part, gc_s.at[i, o], gc_r.at[i, o], me).wait_recv()

    def compute(v, first, stop):
        def body(g, carry):
            ts = [first + g * CHAIN + u for u in range(CHAIN)]
            inner = []
            for t in ts:
                picked = x[src[t], :, :, v].reshape(width, width)
                inner.append(jnp.dot(left[t], picked, preferred_element_type=jnp.float32).astype(jnp.bfloat16))
            outer = [lax.dot_general(a, right[t], (((1,), (1,)), ((), ())), preferred_element_type=jnp.float32)
                     for a, t in zip(inner, ts)]
            for a, t in zip(outer, ts):
                scaled = (a * (coef[t] * factor)).reshape(sums.shape[1:])
                sums[t] = sums[prev[t]] + scaled
            return carry

        lax.fori_loop(0, (stop - first) // CHAIN, body, 0)

    def core_start(v):
        for s in range(sectors):
            end = last[s]
            acc[v, pl.ds(s * half, half)] = sums[end, :, core]
            cbuf[v, pl.ds(s * half, half)] = sums[end, :, 1 - core]
        return start(send(cbuf.at[v], crecv.at[v], rc_s.at[v], rc_r.at[v], at(pz, py, 1 - core)))

    order = list(range(1, na)) + [0]

    def y_start(v, copy):
        copy.wait_recv()
        for i in order:
            z = up(pz, i, na)
            for o in range(1, nb):
                k = z * nb + up(py, o, nb)
                ysend[v, i, o] = (acc[v, k] + crecv[v, k]).astype(jnp.bfloat16)
                start(send(ysend.at[v, i, o], yrecv.at[v, i, o], ry_s.at[v, i, o], ry_r.at[v, i, o],
                           at(pz, up(py, o, nb), core)))

    def z_start(v):
        for i in order:
            z = up(pz, i, na)
            k = z * nb + py
            total = acc[v, k] + crecv[v, k]
            for o in range(1, nb):
                send(ysend.at[v, i, o], yrecv.at[v, i, o], ry_s.at[v, i, o], ry_r.at[v, i, o], me).wait_recv()
                total = total + yrecv[v, i, o].astype(jnp.float32)
            if i == 0:
                sigma[v] = total
            else:
                zsend[v, i] = total.astype(jnp.bfloat16)
                start(send(zsend.at[v, i], zrecv.at[v, i], rz_s.at[v, i], rz_r.at[v, i], at(z, py, core)))

    def finish(v):
        total = sigma[v]
        for i in range(1, na):
            send(zsend.at[v, i], zrecv.at[v, i], rz_s.at[v, i], rz_r.at[v, i], me).wait_recv()
            total = total + zrecv[v, i].astype(jnp.float32)
        sigma[v] = total

    mid = terms // CHAIN // 2 * CHAIN
    waiting = None
    for v in range(nvec):
        compute(v, 0, mid)
        if waiting is not None:
            y_start(v - 1, waiting)
        compute(v, mid, terms)
        waiting = core_start(v)
    y_start(nvec - 1, waiting)

    wide = [x[chip // half, lax.rem(chip, half), core, v].astype(jnp.float32) for v in range(nvec)]

    def lanes(value):
        line = jnp.sum(value, axis=0, keepdims=True)
        return functools.reduce(jnp.add, [line[:, j:j + 128] for j in range(0, width, 128)])

    pbuf[...] = jnp.zeros(pbuf.shape, jnp.float32)
    for v in range(nvec):
        pbuf[pl.ds(nvec * nvec + v, 1)] = lanes(wide[v] * wide[v])
    for v in range(nvec):
        z_start(v)
    for v in range(nvec):
        finish(v)
        for i in range(nvec):
            pbuf[pl.ds(i * nvec + v, 1)] = lanes(wide[i] * sigma[v])

    def small(step):
        return send(pbuf, precv.at[step], p_s.at[step], p_r.at[step], up(me, step, n))

    def put(step, carry):
        small(step).start()
        return carry

    def done(step, carry):
        small(step).wait_send()
        return carry

    lax.fori_loop(1, n, put, 0)
    precv[0] = pbuf[...]

    def arrive(step, carry):
        small(step).wait_recv()
        return carry

    lax.fori_loop(1, n, arrive, 0)

    def add(j, total):
        return total + precv[up(me, n - j, n)]

    total = lax.fori_loop(0, n, add, jnp.zeros(pbuf.shape, jnp.float32))
    whole = jnp.sum(total, axis=1, keepdims=True)
    norm = [whole[nvec * nvec + v:nvec * nvec + v + 1] for v in range(nvec)]
    for v in range(nvec):
        theta = whole[v * nvec + v:v * nvec + v + 1] / norm[v]
        residual[v] = sigma[v] - theta * wide[v]
    row = lax.broadcasted_iota(jnp.int32, (nvec, nvec), 0)
    col = lax.broadcasted_iota(jnp.int32, (nvec, nvec), 1)
    table = jnp.zeros((nvec, nvec), jnp.float32)
    for i in range(nvec):
        for j in range(nvec):
            value = whole[i * nvec + j:i * nvec + j + 1] / jnp.sqrt(norm[i] * norm[j])
            table = jnp.where((row == i) & (col == j), value, table)
    subspace[...] = table
    lax.fori_loop(1, n, done, 0)
    for copy in sent:
        copy.wait_send()


def local(n, vectors, left_ops, right_ops, coefficient, source, target):
    nvec, rows, width = vectors.shape
    terms = left_ops.shape[0]
    sectors = rows * n // width
    na, nb = axis_sizes(n)
    half = n // sectors // 2
    chips = na * nb
    packed = -(-(nvec * nvec + nvec) // 8) * 8
    dma = pltpu.SemaphoreType.DMA
    bf16, f32 = jnp.bfloat16, jnp.float32
    smem = pl.BlockSpec(memory_space=pltpu.SMEM)
    anywhere = pl.BlockSpec(memory_space=pl.ANY)
    vmem = pl.BlockSpec(memory_space=pltpu.VMEM)
    flops = 4 * nvec * terms * width ** 3
    return pl.pallas_call(
        functools.partial(kernel, n, na, nb, nvec, rows, width, sectors, terms),
        out_shape=(jax.ShapeDtypeStruct((nvec, rows, width), f32),
                   jax.ShapeDtypeStruct((nvec, rows, width), f32),
                   jax.ShapeDtypeStruct((nvec, nvec), f32)),
        in_specs=[smem, smem, smem, anywhere, anywhere, anywhere],
        out_specs=(vmem, vmem, vmem),
        scratch_shapes=[
            pltpu.VMEM((sectors, half, 2, nvec, rows, width), bf16),
            pltpu.VMEM((terms, width, width), bf16),
            pltpu.VMEM((terms, width, width), bf16),
            pltpu.VMEM((terms + 1, half, 2, rows, width), f32),
            pltpu.VMEM((nvec, chips, rows, width), f32),
            pltpu.VMEM((nvec, chips, rows, width), f32),
            pltpu.VMEM((nvec, chips, rows, width), f32),
            pltpu.VMEM((nvec, na, nb, rows, width), bf16),
            pltpu.VMEM((nvec, na, nb, rows, width), bf16),
            pltpu.VMEM((nvec, na, rows, width), bf16),
            pltpu.VMEM((nvec, na, rows, width), bf16),
            pltpu.VMEM((packed, 128), f32),
            pltpu.VMEM((n, packed, 128), f32),
            pltpu.SMEM((terms,), jnp.int32),
            pltpu.SMEM((sectors,), jnp.int32),
            dma((3,)),
            dma((na,)), dma((na,)),
            dma((na, nb)), dma((na, nb)),
            dma((na, nb)), dma((na, nb)),
            dma((nvec,)), dma((nvec,)),
            dma((nvec, na, nb)), dma((nvec, na, nb)),
            dma((nvec, na)), dma((nvec, na)),
            dma((n,)), dma((n,)),
        ],
        compiler_params=pltpu.CompilerParams(
            collective_id=0, has_side_effects=True, vmem_limit_bytes=52 * 2 ** 20),
        cost_estimate=pl.CostEstimate(
            flops=flops, bytes_accessed=4 * terms * width ** 2, transcendentals=0),
    )(coefficient, source, target, vectors, left_ops, right_ops)


def solution(mesh):
    n = mesh.shape["term"]
    in_specs = (
        P("group", "term", None),
        P(("group", "term"), None, None),
        P(("group", "term"), None, None),
        P(("group", "term")),
        P(("group", "term")),
        P(("group", "term")),
    )
    out_specs = (P("group", "term", None), P("group", "term", None), P("group", None))
    return jax.shard_map(functools.partial(local, n), mesh=mesh, in_specs=in_specs,
                         out_specs=out_specs, check_vma=False)
```

```python
import functools

import jax
import jax.numpy as jnp
from jax import lax
from jax.experimental import pallas as pl
from jax.experimental.pallas import tpu as pltpu
from jax.sharding import PartitionSpec as P

CHAIN = 4
ORDER = (
    "O0", "O1", "Z0", "O2", "Y0", "Z1", "A0", "C0", "Y1",
    "Z2", "D0", "S0", "A1", "C1", "Y2", "P0", "D1", "S1",
    "A2", "P1", "C2", "Q0", "D2", "S2", "P2", "Q1", "Q2",
)


def axis_sizes(n):
    chips = n // 2
    inner = 1
    while (inner * 2) ** 2 <= chips:
        inner *= 2
    return chips // inner, inner


def kernel(n, na, nb, nvec, rows, width, sectors, terms,
           coef_in, src_in, tgt_in, vec_in, left_in, right_in,
           sigma, residual, subspace,
           x, left, right, sums, acc, cbuf, crecv, ysend, yrecv, zsend, zrecv, pbuf, precv,
           coef, src, tgt, prev, last,
           load_sem, gz_s, gz_r, gy_s, gy_r, gc_s, gc_r,
           rc_s, rc_r, ry_s, ry_r, rz_s, rz_r, p_s, p_r):
    me = lax.axis_index("term")
    core = lax.rem(me, 2)
    chip = lax.div(me, 2)
    py = lax.rem(chip, nb)
    pz = lax.div(chip, nb)
    half = n // sectors // 2
    factor = sectors / (terms * n)

    def at(z, y, c):
        return (z * nb + y) * 2 + c

    def up(value, step, size):
        return lax.rem(value + step, size)

    def send(source, target, send_sem, recv_sem, device):
        copy = pltpu.make_async_remote_copy(
            src_ref=source, dst_ref=target, send_sem=send_sem, recv_sem=recv_sem,
            device_id={"term": device}, device_id_type=pl.DeviceIdType.MESH)
        return copy

    mine = [x[v].at[chip // half, lax.rem(chip, half), core] for v in range(nvec)]
    own = [pltpu.make_async_copy(vec_in.at[v], mine[v], load_sem.at[5 + v]) for v in range(nvec)]
    for copy in own:
        copy.start()
    scalars = [pltpu.make_async_copy(src_ref=a, dst_ref=b, sem=load_sem.at[2 + j])
               for j, (a, b) in enumerate(((coef_in, coef), (src_in, src), (tgt_in, tgt)))]
    for copy in scalars:
        copy.start()
    loads = [pltpu.make_async_copy(left_in, left, load_sem.at[0]),
             pltpu.make_async_copy(right_in, right, load_sem.at[1])]
    for copy in loads:
        copy.start()

    barrier = pltpu.get_barrier_semaphore()

    def greet(step, carry):
        pl.semaphore_signal(barrier, inc=1, device_id={"term": up(me, step, n)},
                            device_id_type=pl.DeviceIdType.MESH)
        return carry

    lax.fori_loop(1, n, greet, 0)

    for copy in scalars:
        copy.wait()

    ends = tuple(jnp.int32(terms) for _ in range(sectors))

    def link(t, ends):
        target = tgt[t]
        before = jnp.int32(terms)
        for s in range(sectors):
            before = jnp.where(target == s, ends[s], before)
        prev[t] = before
        return tuple(jnp.where(target == s, t, ends[s]) for s in range(sectors))

    ends = lax.fori_loop(0, terms, link, ends)
    for s in range(sectors):
        last[s] = ends[s]
    sums[terms] = jnp.zeros(sums.shape[1:], jnp.float32)

    for copy in own:
        copy.wait()
    pl.semaphore_wait(barrier, n - 1)

    def block(v, z, y, c):
        k = z * nb + y
        return x[v].at[lax.div(k, half), lax.rem(k, half), c]

    sent = []

    def start(copy):
        copy.start()
        sent.append(copy)
        return copy

    def own_start(v):
        part = block(v, pz, py, core)
        for o in range(1, na):
            start(send(part, part, gz_s.at[v, o], gz_r.at[v, o], at(up(pz, o, na), py, core)))
        to_y_and_core(v, pz, 0)

    def to_y_and_core(v, z, i):
        part = block(v, z, py, core)
        for o in range(1, nb):
            start(send(part, part, gy_s.at[v, i, o], gy_r.at[v, i, o], at(pz, up(py, o, nb), core)))
        start(send(part, part, gc_s.at[v, i, 0], gc_r.at[v, i, 0], at(pz, py, 1 - core)))

    def z_arrivals(v):
        for i in range(1, na):
            z = up(pz, na - i, na)
            part = block(v, z, py, core)
            send(part, part, gz_s.at[v, i], gz_r.at[v, i], me).wait_recv()
            to_y_and_core(v, z, i)

    def y_arrivals(v):
        for i in range(na):
            z = up(pz, na - i, na)
            for o in range(1, nb):
                part = block(v, z, up(py, nb - o, nb), core)
                send(part, part, gy_s.at[v, i, o], gy_r.at[v, i, o], me).wait_recv()
                start(send(part, part, gc_s.at[v, i, o], gc_r.at[v, i, o], at(pz, py, 1 - core)))

    def core_arrivals(v):
        for i in range(na):
            for o in range(nb):
                part = block(v, up(pz, na - i, na), up(py, nb - o, nb), 1 - core)
                send(part, part, gc_s.at[v, i, o], gc_r.at[v, i, o], me).wait_recv()

    def compute(v, first, stop):
        def body(g, carry):
            ts = [first + g * CHAIN + u for u in range(CHAIN)]
            inner = []
            for t in ts:
                picked = x[v][src[t]].reshape(width, width)
                inner.append(jnp.dot(left[t], picked, preferred_element_type=jnp.float32).astype(jnp.bfloat16))
            outer = [lax.dot_general(a, right[t], (((1,), (1,)), ((), ())), preferred_element_type=jnp.float32)
                     for a, t in zip(inner, ts)]
            for a, t in zip(outer, ts):
                scaled = (a * (coef[t] * factor)).reshape(sums.shape[1:])
                sums[t] = sums[prev[t]] + scaled
            return carry

        lax.fori_loop(0, (stop - first) // CHAIN, body, 0)

    def core_start(v):
        for s in range(sectors):
            end = last[s]
            acc[v, pl.ds(s * half, half)] = sums[end, :, core]
            cbuf[v, pl.ds(s * half, half)] = sums[end, :, 1 - core]
        start(send(cbuf.at[v], crecv.at[v], rc_s.at[v], rc_r.at[v], at(pz, py, 1 - core)))

    order = list(range(1, na)) + [0]

    def y_start(v):
        send(cbuf.at[v], crecv.at[v], rc_s.at[v], rc_r.at[v], me).wait_recv()
        for i in order:
            z = up(pz, i, na)
            for o in range(1, nb):
                k = z * nb + up(py, o, nb)
                ysend[v, i, o] = (acc[v, k] + crecv[v, k]).astype(jnp.bfloat16)
                start(send(ysend.at[v, i, o], yrecv.at[v, i, o], ry_s.at[v, i, o], ry_r.at[v, i, o],
                           at(pz, up(py, o, nb), core)))

    def z_start(v):
        for i in order:
            z = up(pz, i, na)
            k = z * nb + py
            total = acc[v, k] + crecv[v, k]
            for o in range(1, nb):
                send(ysend.at[v, i, o], yrecv.at[v, i, o], ry_s.at[v, i, o], ry_r.at[v, i, o], me).wait_recv()
                total = total + yrecv[v, i, o].astype(jnp.float32)
            if i == 0:
                sigma[v] = total
            else:
                zsend[v, i] = total.astype(jnp.bfloat16)
                start(send(zsend.at[v, i], zrecv.at[v, i], rz_s.at[v, i], rz_r.at[v, i], at(z, py, core)))

    def finish(v):
        total = sigma[v]
        for i in range(1, na):
            send(zsend.at[v, i], zrecv.at[v, i], rz_s.at[v, i], rz_r.at[v, i], me).wait_recv()
            total = total + zrecv[v, i].astype(jnp.float32)
        sigma[v] = total

    mid = terms // CHAIN // 2 * CHAIN
    steps = {"O": own_start, "Z": z_arrivals, "Y": y_arrivals, "A": core_arrivals, "S": core_start,
             "P": y_start, "Q": z_start, "C": lambda v: compute(v, 0, mid), "D": lambda v: compute(v, mid, terms)}
    if nvec == 3:
        plan = ORDER
    else:
        plan = [step + str(v) for v in range(nvec) for step in "OZYACDSPQ"]
    plan = list(plan)
    first = [step[0] for step in plan].index("C")
    for j, step in enumerate(plan):
        if j == first:
            for copy in loads:
                copy.wait()
        steps[step[0]](int(step[1:]))

    wide = [mine[v][...].astype(jnp.float32) for v in range(nvec)]

    def lanes(value):
        line = jnp.sum(value, axis=0, keepdims=True)
        return functools.reduce(jnp.add, [line[:, j:j + 128] for j in range(0, width, 128)])

    pbuf[...] = jnp.zeros(pbuf.shape, jnp.float32)
    for v in range(nvec):
        pbuf[pl.ds(nvec * nvec + v, 1)] = lanes(wide[v] * wide[v])
    for v in range(nvec):
        finish(v)
        for i in range(nvec):
            pbuf[pl.ds(i * nvec + v, 1)] = lanes(wide[i] * sigma[v])

    def small(step):
        return send(pbuf, precv.at[step], p_s.at[step], p_r.at[step], up(me, step, n))

    def put(step, carry):
        small(step).start()
        return carry

    def done(step, carry):
        small(step).wait_send()
        return carry

    lax.fori_loop(1, n, put, 0)
    precv[0] = pbuf[...]

    def arrive(step, carry):
        small(step).wait_recv()
        return carry

    lax.fori_loop(1, n, arrive, 0)

    def add(j, total):
        return total + precv[up(me, n - j, n)]

    total = lax.fori_loop(0, n, add, jnp.zeros(pbuf.shape, jnp.float32))
    whole = jnp.sum(total, axis=1, keepdims=True)
    norm = [whole[nvec * nvec + v:nvec * nvec + v + 1] for v in range(nvec)]
    for v in range(nvec):
        theta = whole[v * nvec + v:v * nvec + v + 1] / norm[v]
        residual[v] = sigma[v] - theta * wide[v]
    row = lax.broadcasted_iota(jnp.int32, (nvec, nvec), 0)
    col = lax.broadcasted_iota(jnp.int32, (nvec, nvec), 1)
    table = jnp.zeros((nvec, nvec), jnp.float32)
    for i in range(nvec):
        for j in range(nvec):
            value = whole[i * nvec + j:i * nvec + j + 1] / jnp.sqrt(norm[i] * norm[j])
            table = jnp.where((row == i) & (col == j), value, table)
    subspace[...] = table
    lax.fori_loop(1, n, done, 0)
    for copy in sent:
        copy.wait_send()


def local(n, vectors, left_ops, right_ops, coefficient, source, target):
    nvec, rows, width = vectors.shape
    terms = left_ops.shape[0]
    sectors = rows * n // width
    na, nb = axis_sizes(n)
    half = n // sectors // 2
    chips = na * nb
    packed = -(-(nvec * nvec + nvec) // 8) * 8
    dma = pltpu.SemaphoreType.DMA
    bf16, f32 = jnp.bfloat16, jnp.float32
    anywhere = pl.BlockSpec(memory_space=pltpu.HBM)
    vmem = pl.BlockSpec(memory_space=pltpu.VMEM)
    flops = 4 * nvec * terms * width ** 3
    return pl.pallas_call(
        functools.partial(kernel, n, na, nb, nvec, rows, width, sectors, terms),
        out_shape=(jax.ShapeDtypeStruct((nvec, rows, width), f32),
                   jax.ShapeDtypeStruct((nvec, rows, width), f32),
                   jax.ShapeDtypeStruct((nvec, nvec), f32)),
        in_specs=[anywhere] * 6,
        out_specs=(vmem, vmem, vmem),
        scratch_shapes=[
            tuple(pltpu.VMEM((sectors, half, 2, rows, width), bf16) for _ in range(nvec)),
            pltpu.VMEM((terms, width, width), bf16),
            pltpu.VMEM((terms, width, width), bf16),
            pltpu.VMEM((terms + 1, half, 2, rows, width), f32),
            pltpu.VMEM((nvec, chips, rows, width), f32),
            pltpu.VMEM((nvec, chips, rows, width), f32),
            pltpu.VMEM((nvec, chips, rows, width), f32),
            pltpu.VMEM((nvec, na, nb, rows, width), bf16),
            pltpu.VMEM((nvec, na, nb, rows, width), bf16),
            pltpu.VMEM((nvec, na, rows, width), bf16),
            pltpu.VMEM((nvec, na, rows, width), bf16),
            pltpu.VMEM((packed, 128), f32),
            pltpu.VMEM((n, packed, 128), f32),
            pltpu.SMEM((terms,), f32),
            pltpu.SMEM((terms,), jnp.int32),
            pltpu.SMEM((terms,), jnp.int32),
            pltpu.SMEM((terms,), jnp.int32),
            pltpu.SMEM((sectors,), jnp.int32),
            dma((5 + nvec,)),
            dma((nvec, na)), dma((nvec, na)),
            dma((nvec, na, nb)), dma((nvec, na, nb)),
            dma((nvec, na, nb)), dma((nvec, na, nb)),
            dma((nvec,)), dma((nvec,)),
            dma((nvec, na, nb)), dma((nvec, na, nb)),
            dma((nvec, na)), dma((nvec, na)),
            dma((n,)), dma((n,)),
        ],
        compiler_params=pltpu.CompilerParams(
            collective_id=0, has_side_effects=True, vmem_limit_bytes=52 * 2 ** 20),
        cost_estimate=pl.CostEstimate(
            flops=flops, bytes_accessed=4 * terms * width ** 2, transcendentals=0),
    )(coefficient, source, target, vectors, left_ops, right_ops)


def solution(mesh):
    n = mesh.shape["term"]
    in_specs = (
        P("group", "term", None),
        P(("group", "term"), None, None),
        P(("group", "term"), None, None),
        P(("group", "term")),
        P(("group", "term")),
        P(("group", "term")),
    )
    out_specs = (P("group", "term", None), P("group", "term", None), P("group", None))
    return jax.shard_map(functools.partial(local, n), mesh=mesh, in_specs=in_specs,
                         out_specs=out_specs, check_vma=False)
```
